32 devices in a mesh: groups: 1, dom: 8 (over z, y), chan: 2 (over x), sub: 2 (over core).
Axes of the slice: x: 2, y: 2, z: 4, core: 2. Of those that a mesh axis runs over, the one named last changes fastest.
Arguments:
- y_last: bfloat16 [2, 128, 8192], P(None, 'chan', ('groups', 'dom', 'sub')), may hold values from -6 to 6
- dy_last: bfloat16 [2, 128, 8192], P(None, 'chan', ('groups', 'dom', 'sub')), may hold values from -6 to 6
- weights: bfloat16 [2, 2, 128, 128], replicated, may hold values from -0.5 to 0.5
- tile_vals: bfloat16 [64, 8, 128, 128], P(('groups', 'dom', 'sub')), may hold values from -0.1875 to 0.1875
- tile_cols: int32 [64, 8], P(('groups', 'dom', 'sub')), may hold values from 0 to 7, as said below
- tile_mask: int32 [64, 8], P(('groups', 'dom', 'sub')), may hold values from 0 to 1, as said below
- send_rows: int32 [16, 16, 32], P(('groups', 'dom', 'sub')), may hold values from 0 to 511, as said below
- send_count: int32 [16, 16], P(('groups', 'dom', 'sub')), may hold values from 0 to 32, as said below
Outputs:
- input_grads: bfloat16 [2, 128, 8192], P(None, 'chan', ('groups', 'dom', 'sub'))
- weight_grads: float32 [2, 2, 128, 128], P('groups', None, 'chan')
The draws below stay inside these ranges and needn't reach their ends.
Inputs may be any that keep to these rules, and one draw needn't show every extreme that they name: The 8 entries of one row of tile_cols are distinct; slot 0 of row q * 4 + r names column block r, the block's own rows. `tile_mask`: in each row the live slots come first and slot 0 is live. The first send_count[p, q] entries of send_rows[p, q] are distinct. send_count[p, p] is 0; in every draw some block q receives 32 rows from every other block.
All inputs are finite; a program needn't handle non-finite values.
Results may differ from the reference program's by a relative error of at most 0.0085.
Values may be sent and summed in bfloat16 or wider, within the bound.
A program may use at most 64 MiB of HBM per device.

```python
import math
from functools import partial
import jax
import jax.numpy as jnp
from jax import lax

C = 128
CGROUPS = 2
LAYERS = 2
TB = 128
K = 8
R = 512
B = 32
NDEV = 16
ROWS = 8192
RB = 4
NCB = 8


def draw_tile_cols(key, part):
    key = jax.random.fold_in(key, 11)
    row_count = NDEV * RB
    scores = jax.random.randint(key, (row_count, NCB), 0, 2 ** 20, dtype=jnp.int32) * NCB
    columns = jnp.arange(NCB, dtype=jnp.int32)[None, :]
    scores = scores + columns
    own_block = (jnp.arange(row_count, dtype=jnp.int32) % RB)[:, None]
    scores = jnp.where(columns == own_block, -2, scores)
    first_row = jnp.arange(row_count, dtype=jnp.int32)[:, None] == 0
    scores = jnp.where(first_row & (columns == NCB - 1), -1, scores)
    order = jnp.argsort(scores, axis=1, stable=True)
    return order[:, :K].astype(jnp.int32)


def draw_tile_mask(key, part):
    key = jax.random.fold_in(key, 12)
    key_count, key_full, key_level = jax.random.split(key, 3)
    row_count = NDEV * RB
    level = jax.random.randint(key_level, (NDEV,), 0, K // 2 + 1, dtype=jnp.int32)
    counts = jax.random.randint(key_count, (row_count,), 1, K + 1, dtype=jnp.int32) + jnp.repeat(level, RB)
    counts = jnp.minimum(counts, K)
    full_block = jax.random.randint(key_full, (NDEV,), 0, RB, dtype=jnp.int32)
    block_of = jnp.arange(row_count, dtype=jnp.int32) % RB
    device_of = jnp.arange(row_count, dtype=jnp.int32) // RB
    counts = jnp.where(block_of == full_block[device_of], K, counts)
    sparse_row = (device_of == 0) & (block_of == (full_block[0] + 1) % RB)
    counts = jnp.where(sparse_row, 1, counts)
    slots = jnp.arange(K, dtype=jnp.int32)[None, :]
    return (slots < counts[:, None]).astype(jnp.int32)


def draw_send_rows(key, part):
    key = jax.random.fold_in(key, 14)
    scores = jax.random.randint(key, (NDEV, NDEV, R), 0, 2 ** 18, dtype=jnp.int32) * R
    row_iota = jnp.arange(R, dtype=jnp.int32)[None, None, :]
    scores = scores + row_iota
    pair_mask = (jnp.arange(NDEV, dtype=jnp.int32)[:, None, None] == 0) & (jnp.arange(NDEV, dtype=jnp.int32)[None, :, None] == 1)
    scores = jnp.where(pair_mask & (row_iota == R - 1), -1, scores)
    scores = jnp.where(pair_mask & (row_iota == 0), -2, scores)
    order = jnp.argsort(scores, axis=2, stable=True)
    return order[:, :, :B].astype(jnp.int32)


def draw_send_count(key, part):
    key = jax.random.fold_in(key, 13)
    key_base, key_level, key_hot = jax.random.split(key, 3)
    base = jax.random.randint(key_base, (NDEV, NDEV), 0, B + 1, dtype=jnp.int32)
    level = jax.random.randint(key_level, (NDEV,), 1, 4, dtype=jnp.int32)
    counts = jnp.minimum(base * level[None, :] // 2, B)
    hottest = jax.random.randint(key_hot, (), 0, NDEV, dtype=jnp.int32)
    target = jnp.arange(NDEV, dtype=jnp.int32)[None, :]
    counts = jnp.where(target == hottest, B, counts)
    source = jnp.arange(NDEV, dtype=jnp.int32)[:, None]
    counts = jnp.where(source == target, 0, counts)
    return counts.astype(jnp.int32)


def steps_of(stream_key, dims, pieces, smallest, high):
    def one(axis_at, blocks):
        draws = jax.random.uniform(jax.random.fold_in(jax.random.fold_in(stream_key, 6), axis_at), (blocks,), jnp.float32, smallest / len(pieces), high / len(pieces))
        return jnp.repeat(jnp.exp(draws), dims[axis_at] // blocks).reshape((-1,) + (1,) * (len(dims) - axis_at - 1))

    factor_of = one(*pieces[0])
    for cut in pieces[1:]:
        factor_of = factor_of * one(*cut)
    return factor_of


def noise(stream_key, shape, scale, reach, cuts=(), kind=jnp.bfloat16):
    entries = scale * jax.random.normal(stream_key, shape, jnp.float32)
    if cuts:
        entries = entries * steps_of(stream_key, shape, cuts, -0.22, 0.18)
    return jnp.clip(entries, -reach, reach).astype(kind)


def setup_inputs(seed: int = 0, part: int = 0) -> dict:
    arg_keys = jax.random.split(jax.random.key(seed), 9)
    own_keys = jax.random.split(jax.random.fold_in(arg_keys[8], part), 9)
    return {
        "y_last": noise(own_keys[0], (CGROUPS, C, ROWS), 1.0, 6.0, ((1, 2), (2, 16))),
        "dy_last": noise(own_keys[1], (CGROUPS, C, ROWS), 1.0, 6.0, ((1, 2), (2, 16))),
        "weights": noise(arg_keys[2], (LAYERS, CGROUPS, C, C), C ** -0.5, 0.5),
        "tile_vals": noise(own_keys[3], (NDEV * RB, K, TB, TB), (TB * K) ** -0.5, 0.1875, ((0, 16),)),
        "tile_cols": draw_tile_cols(jax.random.fold_in(jax.random.fold_in(arg_keys[8], part), 71), part),
        "tile_mask": draw_tile_mask(jax.random.fold_in(jax.random.fold_in(arg_keys[8], part), 71), part),
        "send_rows": draw_send_rows(jax.random.fold_in(jax.random.fold_in(arg_keys[8], part), 71), part),
        "send_count": draw_send_count(jax.random.fold_in(jax.random.fold_in(arg_keys[8], part), 71), part),
    }


def silu_slope(value):
    sigmoid = jax.nn.sigmoid(value)
    return sigmoid * (1.0 + value * (1.0 - sigmoid))

def propagate(feature, tile_vals, tile_cols, tile_mask, send_rows, send_count):
    tile_grid = tile_vals.reshape(NDEV, RB, K, TB, TB)
    col_grid = tile_cols.reshape(NDEV, RB, K)
    mask_grid = tile_mask.reshape(NDEV, RB, K)
    slot_index = jnp.arange(B, dtype=jnp.int32)
    sources = jnp.arange(NDEV, dtype=jnp.int32)

    def one_block(block):
        own_part = lax.dynamic_slice_in_dim(feature, block * R, R, 1)
        chosen = lax.dynamic_index_in_dim(send_rows, block, 1, keepdims=False)
        counts = lax.dynamic_index_in_dim(send_count, block, 1, keepdims=False)
        halo_index = (sources[:, None] * R + chosen).reshape(-1).astype(jnp.int32)
        live_mask = (slot_index[None, :] < counts[:, None]).reshape(-1)
        halo_part = jnp.where(live_mask[None, :], feature[:, halo_index], jnp.zeros((), feature.dtype))
        extended = jnp.concatenate([own_part, halo_part], axis=1).reshape(C, NCB, TB)
        picked = extended[:, col_grid[block]] * mask_grid[block][None, :, :, None].astype(feature.dtype)
        result = jnp.einsum('crkj,rkji->cri', picked, tile_grid[block].astype(feature.dtype))
        return result.reshape(C, R)
    blocks = lax.map(one_block, sources)
    return jnp.transpose(blocks, (1, 0, 2)).reshape(C, NDEV * R)

def reference(y_last, dy_last, weights, tile_vals, tile_cols, tile_mask, send_rows, send_count):
    moving = partial(propagate, tile_vals=tile_vals, tile_cols=tile_cols, tile_mask=tile_mask, send_rows=send_rows, send_count=send_count)

    def forward_pass(feature):
        return moving(feature.astype(jnp.float32))

    def backward_pass(gradient):
        start_point = jnp.zeros(gradient.shape, jnp.float32)
        _, pullback = jax.vjp(moving, start_point)
        return pullback(gradient.astype(jnp.float32))[0]
    state_one = y_last[0]
    state_two = y_last[1]
    grad_one = dy_last[0].astype(jnp.float32)
    grad_two = dy_last[1].astype(jnp.float32)
    collected = []
    for layer_index in reversed(range(LAYERS)):
        first = weights[layer_index, 0]
        second = weights[layer_index, 1]
        message_two = forward_pass(state_one).astype(jnp.bfloat16)
        linear_two = jnp.dot(second.T, message_two, preferred_element_type=jnp.float32)
        input_two = (state_two.astype(jnp.float32) - jax.nn.silu(linear_two)).astype(jnp.bfloat16)
        message_one = forward_pass(input_two).astype(jnp.bfloat16)
        linear_one = jnp.dot(first.T, message_one, preferred_element_type=jnp.float32)
        slope_two = (grad_two * silu_slope(linear_two)).astype(jnp.bfloat16)
        back_two = jnp.dot(second, slope_two, preferred_element_type=jnp.float32).astype(jnp.bfloat16)
        grad_one = grad_one + backward_pass(back_two)
        slope_one = (grad_one * silu_slope(linear_one)).astype(jnp.bfloat16)
        back_one = jnp.dot(first, slope_one, preferred_element_type=jnp.float32).astype(jnp.bfloat16)
        grad_two = grad_two + backward_pass(back_one)
        weight_one = jnp.dot(message_one, slope_one.T, preferred_element_type=jnp.float32)
        weight_two = jnp.dot(message_two, slope_two.T, preferred_element_type=jnp.float32)
        collected.insert(0, jnp.stack([weight_one, weight_two]))
        if layer_index > 0:
            state_one = (state_one.astype(jnp.float32) - jax.nn.silu(linear_one)).astype(jnp.bfloat16)
            state_two = input_two
    input_grads = jnp.stack([grad_one, grad_two]).astype(jnp.bfloat16)
    weight_grads = jnp.stack(collected) * (1.0 / math.sqrt(ROWS))
    return (input_grads, weight_grads)
```

```python
import functools
import math

import jax
import jax.numpy as jnp
from jax import lax
from jax.experimental import pallas as pl
from jax.experimental.pallas import tpu as pltpu
from jax.sharding import PartitionSpec as P

MESH = pl.DeviceIdType.MESH
F32 = jnp.float32
BF16 = jnp.bfloat16


def sigmoid(value):
    return 1.0 / (1.0 + jnp.exp(-value))


def dot(a, b):
    return jnp.dot(a, b, preferred_element_type=F32)


def dot_nt(a, b):
    return lax.dot_general(a, b, (((1,), (1,)), ((), ())), preferred_element_type=F32)


def dot_tn(a, b):
    return lax.dot_general(a, b, (((0,), (0,)), ((), ())), preferred_element_type=F32)


def kernel(
    blocks, subs, chans, slots_each, rows_each, factor,
    y_ref, dy_ref, weights_ref, tiles_ref, cols_ref, mask_ref, slot_ref,
    grads_ref, wgrads_ref,
    full, gather, scatter, pick, put, ext, out, back, ret, wpart, wsum, wred, wall, square, wide, held, msgs, slopes,
    chan_send, chan_recv, send_sem, recv_sem,
):
    layers = weights_ref.shape[0]
    _, part, rows = y_ref.shape
    channels = part * chans
    row_blocks, tile_slots = cols_ref.shape
    tile = tiles_ref.shape[-1]
    col_blocks = ext.shape[1] // tile
    my_sub = lax.axis_index("sub")
    me = lax.axis_index("dom") * subs + my_sub
    my_chan = lax.axis_index("chan")

    def block_of(step):
        peer = lax.rem(me + step, blocks)
        return peer, {"dom": peer // subs, "sub": lax.rem(peer, subs)}

    def chan_of(step):
        return {"chan": lax.rem(my_chan + step, chans)}

    barrier = pltpu.get_barrier_semaphore()

    @pl.loop(1, blocks)
    def _(step):
        pl.semaphore_signal(barrier, inc=1, device_id=block_of(step)[1], device_id_type=MESH)

    for step in range(1, chans):
        pl.semaphore_signal(barrier, inc=1, device_id=chan_of(step), device_id_type=MESH)
    pl.semaphore_wait(barrier, blocks - 1 + chans - 1)

    mine = pl.ds(pl.multiple_of(my_chan * part, part), part)

    def chan_copy(field, step):
        source = y_ref.at[field] if field < 2 else dy_ref.at[field - 2]
        return pltpu.make_async_remote_copy(
            src_ref=source,
            dst_ref=full.at[field, mine],
            send_sem=chan_send.at[field, step],
            recv_sem=chan_recv.at[field, step],
            device_id=chan_of(step),
            device_id_type=MESH,
        )

    order = (0, 1, 3, 2)
    for field in order:
        for step in range(1, chans):
            chan_copy(field, step).start()

    def copy_of(index, source, target, offset, size, spread):
        def one(step):
            peer, device = block_of(step)
            src = source.at[pl.ds(pl.multiple_of(peer * size, size), size)] if spread else source
            return pltpu.make_async_remote_copy(
                src_ref=src,
                dst_ref=target.at[pl.ds(pl.multiple_of(offset + me * size, size), size)],
                send_sem=send_sem.at[index, step],
                recv_sem=recv_sem.at[index, step],
                device_id=device,
                device_id_type=MESH,
            )

        return one

    def start(one):
        @pl.loop(1, blocks)
        def _(step):
            one(step).start()

    def finish(one):
        @pl.loop(1, blocks)
        def _(step):
            one(step).wait()

    own_slots = pl.ds(pl.multiple_of(me * slots_each, slots_each), slots_each)
    own_extended = pl.ds(pl.multiple_of(rows + me * slots_each, slots_each), slots_each)
    blank = jnp.zeros((slots_each, channels), BF16)
    for index in range(2 * layers):
        ext[index, own_extended, :] = blank
        ret[index, own_slots, :] = blank

    halo = blocks * slots_each
    slot_row = slot_ref[...]
    put[...] = (lax.broadcasted_iota(jnp.int32, (rows, halo), 0) == slot_row).astype(F32).astype(BF16)
    for at in range(0, halo, tile):
        column = jnp.broadcast_to(slot_row[:, at : at + tile].astype(F32), (tile, tile)).T
        for row_at in range(0, rows, tile):
            lanes = (lax.broadcasted_iota(jnp.int32, (tile, tile), 1) + row_at).astype(F32)
            pick[at : at + tile, row_at : row_at + tile] = (lanes == column).astype(F32).astype(BF16)

    for row_block in range(row_blocks):
        row_span = slice(row_block * tile, (row_block + 1) * tile)

        def place(col, carry):
            slot = jnp.int32(0)
            live = jnp.int32(0)
            for k in range(tile_slots):
                hit = (cols_ref[row_block, k] == col) & (mask_ref[row_block, k] > 0)
                slot = jnp.where(hit, k, slot)
                live = jnp.where(hit, 1, live)
            block = tiles_ref[row_block, slot].astype(F32) * live.astype(F32)
            span = pl.ds(pl.multiple_of(col * tile, tile), tile)
            scatter[span, row_span] = block.astype(BF16)
            gather[row_span, span] = block.T.astype(BF16)
            return carry

        lax.fori_loop(0, col_blocks, place, 0)

    def arrived(field):
        for step in range(1, chans):
            chan_copy(field, step).wait()
        source = y_ref[field] if field < 2 else dy_ref[field - 2]
        full[field, mine, :] = source
        return full[field].astype(F32).T

    def forward(index):
        return copy_of(index, out.at[index], ext.at[index], rows, slots_each, True)

    def backward(index):
        return copy_of(2 * layers + index, back.at[index], ret.at[index], 0, slots_each, True)

    def send_field(index, field):
        out[index] = dot(pick[...], field).astype(BF16)
        start(forward(index))
        return dot(gather[:, :rows], field)

    def message(index, own):
        finish(forward(index))
        return (own + dot(gather[:, rows:], ext[index, rows:, :])).astype(BF16)

    def send_gradient(index, field):
        back[index] = dot(scatter[rows:, :], field).astype(BF16)
        start(backward(index))
        return dot(scatter[:rows, :], field)

    def returned(index):
        finish(backward(index))
        return dot(put[...], ret[index])

    def weight_part(layer, which, moved, slope):
        square[...] = dot_tn(moved, slope)
        at = (layer * 2 + which) * part
        wpart[at : at + part, :] = square[mine, :]

    used = 2 * layers * part
    if used < wpart.shape[0]:
        wpart[used:, :] = jnp.zeros((wpart.shape[0] - used, channels), F32)

    held[0] = arrived(0)
    held[4] = send_field(0, held[0].astype(BF16))
    held[1] = arrived(1)
    held[3] = arrived(3)
    held[2] = arrived(2)
    moves = 0
    pending = None
    for layer in reversed(range(layers)):
        first = weights_ref[layer, 0]
        second = weights_ref[layer, 1]
        msgs[1] = message(moves, held[4])
        linear_two = dot(msgs[1], second)
        gate_two = sigmoid(linear_two)
        held[5] = gate_two * (1.0 + linear_two * (1.0 - gate_two))
        input_two = (held[1] - linear_two * gate_two).astype(BF16)
        held[1] = input_two.astype(F32)
        held[4] = send_field(moves + 1, input_two)
        if pending is not None:
            held[3] += returned(pending)
        slopes[1] = (held[3] * held[5]).astype(BF16)
        held[2] += send_gradient(moves, dot_nt(slopes[1], second).astype(BF16))
        weight_part(layer, 1, msgs[1], slopes[1])
        msgs[0] = message(moves + 1, held[4])
        linear_one = dot(msgs[0], first)
        gate_one = sigmoid(linear_one)
        held[5] = gate_one * (1.0 + linear_one * (1.0 - gate_one))
        if layer > 0:
            state_one = (held[0] - linear_one * gate_one).astype(BF16)
            held[0] = state_one.astype(F32)
            held[4] = send_field(moves + 2, state_one)
        held[2] += returned(moves)
        slopes[0] = (held[2] * held[5]).astype(BF16)
        held[3] += send_gradient(moves + 1, dot_nt(slopes[0], first).astype(BF16))
        weight_part(layer, 0, msgs[0], slopes[0])
        pending = moves + 1
        moves += 2

    reduce_copy = copy_of(4 * layers, wpart, wsum, 0, rows_each, True)
    start(reduce_copy)
    own_piece = pl.ds(pl.multiple_of(me * rows_each, rows_each), rows_each)
    wsum[own_piece, :] = wpart[own_piece, :]
    wide[...] = held[2].T
    grads_ref[0] = wide[mine, :].astype(BF16)
    finish(reduce_copy)
    total = wsum[:rows_each, :]
    for piece in range(1, blocks):
        total = total + wsum[piece * rows_each : (piece + 1) * rows_each, :]
    wred[...] = total * factor
    spread_copy = copy_of(4 * layers + 1, wred, wall, 0, rows_each, False)
    start(spread_copy)
    wall[own_piece, :] = wred[...]
    wide[...] = (held[3] + returned(pending)).T
    grads_ref[1] = wide[mine, :].astype(BF16)
    finish(spread_copy)
    for layer in range(layers):
        for which in range(2):
            at = (layer * 2 + which) * part
            wgrads_ref[layer, which] = wall[at : at + part, :]


def solution(mesh):
    blocks = mesh.shape["dom"] * mesh.shape["sub"]
    subs = mesh.shape["sub"]
    chans = mesh.shape["chan"]

    def on_device(y_last, dy_last, weights, tile_vals, tile_cols, tile_mask, send_rows, send_count):
        _, part, rows = y_last.shape
        layers = weights.shape[0]
        channels = part * chans
        slots_each = send_rows.shape[2]
        halo = blocks * slots_each
        live = jnp.arange(slots_each, dtype=jnp.int32)[None, :] < send_count[0][:, None]
        slot_row = jnp.where(live, send_rows[0], -1).reshape(1, halo)
        rows_each = max(8, 2 * layers * part // blocks)
        pieces = blocks * rows_each
        exchanges = 4 * layers + 2
        factor = 1.0 / math.sqrt(rows * blocks)
        vmem = pl.BlockSpec(memory_space=pltpu.VMEM)
        smem = pl.BlockSpec(memory_space=pltpu.SMEM)
        return pl.pallas_call(
            functools.partial(kernel, blocks, subs, chans, slots_each, rows_each, factor),
            out_shape=(
                jax.ShapeDtypeStruct(y_last.shape, BF16),
                jax.ShapeDtypeStruct((layers, 2, part, channels), F32),
            ),
            in_specs=[vmem, vmem, vmem, vmem, smem, smem, vmem],
            out_specs=(vmem, vmem),
            scratch_shapes=[
                pltpu.VMEM((4, channels, rows), BF16),
                pltpu.VMEM((rows, rows + halo), BF16),
                pltpu.VMEM((rows + halo, rows), BF16),
                pltpu.VMEM((halo, rows), BF16),
                pltpu.VMEM((rows, halo), BF16),
                pltpu.VMEM((2 * layers, rows + halo, channels), BF16),
                pltpu.VMEM((2 * layers, halo, channels), BF16),
                pltpu.VMEM((2 * layers, halo, channels), BF16),
                pltpu.VMEM((2 * layers, halo, channels), BF16),
                pltpu.VMEM((pieces, channels), F32),
                pltpu.VMEM((pieces, channels), F32),
                pltpu.VMEM((rows_each, channels), F32),
                pltpu.VMEM((pieces, channels), F32),
                pltpu.VMEM((channels, channels), F32),
                pltpu.VMEM((channels, rows), F32),
                pltpu.VMEM((6, rows, channels), F32),
                pltpu.VMEM((2, rows, channels), BF16),
                pltpu.VMEM((2, rows, channels), BF16),
                pltpu.SemaphoreType.DMA((4, chans)),
                pltpu.SemaphoreType.DMA((4, chans)),
                pltpu.SemaphoreType.DMA((exchanges, blocks)),
                pltpu.SemaphoreType.DMA((exchanges, blocks)),
            ],
            compiler_params=pltpu.CompilerParams(
                collective_id=0, has_side_effects=True, vmem_limit_bytes=44 * 1024 * 1024
            ),
        )(y_last, dy_last, weights, tile_vals, tile_cols, tile_mask, slot_row)

    return jax.shard_map(
        on_device,
        mesh=mesh,
        in_specs=(
            P(None, "chan", ("groups", "dom", "sub")),
            P(None, "chan", ("groups", "dom", "sub")),
            P(),
            P(("groups", "dom", "sub"), None, None, None),
            P(("groups", "dom", "sub"), None),
            P(("groups", "dom", "sub"), None),
            P(("groups", "dom", "sub"), None, None),
            P(("groups", "dom", "sub"), None),
        ),
        out_specs=(P(None, "chan", ("groups", "dom", "sub")), P("groups", None, "chan", None)),
        check_vma=False,
    )
```

```python
import functools
import math

import jax
import jax.numpy as jnp
from jax import lax
from jax.experimental import pallas as pl
from jax.experimental.pallas import tpu as pltpu
from jax.sharding import PartitionSpec as P

MESH = pl.DeviceIdType.MESH
F32 = jnp.float32
BF16 = jnp.bfloat16


def sigmoid(value):
    return 1.0 / (1.0 + jnp.exp(-value))


def dot(a, b):
    return jnp.dot(a, b, preferred_element_type=F32)


def dot_nt(a, b):
    return lax.dot_general(a, b, (((1,), (1,)), ((), ())), preferred_element_type=F32)


def dot_tn(a, b):
    return lax.dot_general(a, b, (((0,), (0,)), ((), ())), preferred_element_type=F32)


def kernel(
    blocks, subs, chans, slots_each, rows_each, factor,
    y_hbm, dy_hbm, weights_hbm, tiles_hbm, cols_ref, mask_ref, rows_hbm, count_hbm,
    grads_ref, wgrads_ref,
    full, gather, scatter, pick, put, ext, out, back, ret, wpart, wsum, wred, wall, square, wide, held, msgs, slopes,
    weights_ref, tiles_ref, rows_ref, count_ref, chan_send, chan_recv, send_sem, recv_sem, local_sem,
):
    layers = weights_ref.shape[0]
    _, part, rows = y_hbm.shape
    channels = part * chans
    row_blocks, tile_slots = cols_ref.shape
    tile = tiles_ref.shape[-1]
    col_blocks = ext.shape[1] // tile
    my_sub = lax.axis_index("sub")
    me = lax.axis_index("dom") * subs + my_sub
    my_chan = lax.axis_index("chan")

    def block_of(step):
        peer = lax.rem(me + step, blocks)
        return peer, {"dom": peer // subs, "sub": lax.rem(peer, subs)}

    def chan_of(step):
        return {"chan": lax.rem(my_chan + step, chans)}

    mine = pl.ds(pl.multiple_of(my_chan * part, part), part)

    def source_of(field):
        return y_hbm.at[field] if field < 2 else dy_hbm.at[field - 2]

    rows_in = pltpu.make_async_copy(rows_hbm, rows_ref, local_sem.at[0])
    count_in = pltpu.make_async_copy(count_hbm, count_ref, local_sem.at[1])
    tiles_in = pltpu.make_async_copy(tiles_hbm, tiles_ref, local_sem.at[2])
    weights_in = pltpu.make_async_copy(weights_hbm, weights_ref, local_sem.at[3])
    fields_in = [
        pltpu.make_async_copy(source_of(field), full.at[field, mine], local_sem.at[4 + field])
        for field in range(4)
    ]
    for copy in (rows_in, count_in, *fields_in, tiles_in, weights_in):
        copy.start()

    barrier = pltpu.get_barrier_semaphore()

    @pl.loop(1, blocks)
    def _(step):
        pl.semaphore_signal(barrier, inc=1, device_id=block_of(step)[1], device_id_type=MESH)

    for step in range(1, chans):
        pl.semaphore_signal(barrier, inc=1, device_id=chan_of(step), device_id_type=MESH)
    pl.semaphore_wait(barrier, blocks - 1 + chans - 1)

    def chan_copy(field, step):
        return pltpu.make_async_remote_copy(
            src_ref=source_of(field),
            dst_ref=full.at[field, mine],
            send_sem=chan_send.at[field, step],
            recv_sem=chan_recv.at[field, step],
            device_id=chan_of(step),
            device_id_type=MESH,
        )

    order = (0, 1, 3, 2)
    for field in order:
        for step in range(1, chans):
            chan_copy(field, step).start()

    def copy_of(index, source, target, offset, size, spread):
        def one(step):
            peer, device = block_of(step)
            src = source.at[pl.ds(pl.multiple_of(peer * size, size), size)] if spread else source
            return pltpu.make_async_remote_copy(
                src_ref=src,
                dst_ref=target.at[pl.ds(pl.multiple_of(offset + me * size, size), size)],
                send_sem=send_sem.at[index, step],
                recv_sem=recv_sem.at[index, step],
                device_id=device,
                device_id_type=MESH,
            )

        return one

    def start(one):
        @pl.loop(1, blocks, unroll=3)
        def _(step):
            one(step).start()

    def finish(one):
        @pl.loop(1, blocks, unroll=3)
        def _(step):
            one(step).wait()

    own_slots = pl.ds(pl.multiple_of(me * slots_each, slots_each), slots_each)
    own_extended = pl.ds(pl.multiple_of(rows + me * slots_each, slots_each), slots_each)
    blank = jnp.zeros((slots_each, channels), BF16)
    for index in range(2 * layers):
        ext[index, own_extended, :] = blank
        ret[index, own_slots, :] = blank

    halo = blocks * slots_each
    rows_in.wait()
    count_in.wait()
    slot_at = lax.broadcasted_iota(jnp.int32, (blocks, halo), 1)
    block_at = lax.broadcasted_iota(jnp.int32, (blocks, halo), 0)
    offset = slot_at - block_at * slots_each
    inside = (offset >= 0) & (offset < slots_each)
    within = jnp.sum(jnp.where(inside, offset, 0).astype(F32), axis=0, keepdims=True)
    spread = inside.astype(F32).astype(BF16)
    entry = lax.broadcasted_iota(jnp.int32, (slots_each, halo), 0).astype(F32)
    matching = (entry == within).astype(F32).astype(BF16)
    listed = rows_ref[0]
    high = dot((listed >> 8).astype(F32).astype(BF16), matching)
    low = dot((listed & 255).astype(F32).astype(BF16), matching)
    chosen = jnp.sum(jnp.where(inside, high * 256.0 + low, 0.0), axis=0, keepdims=True)
    counts = jnp.broadcast_to(count_ref[...].astype(F32), (8, blocks)).astype(BF16)
    limit = dot(counts, spread)[0:1]
    slot_row = jnp.where(within < limit, chosen, -1.0)
    for at in range(0, halo, tile):
        column = jnp.broadcast_to(slot_row[:, at : at + tile], (tile, tile)).T
        for row_at in range(0, rows, tile):
            lanes = (lax.broadcasted_iota(jnp.int32, (tile, tile), 1) + row_at).astype(F32)
            pick[at : at + tile, row_at : row_at + tile] = (lanes == column).astype(F32).astype(BF16)

    def arrived(field):
        for step in range(1, chans):
            chan_copy(field, step).wait()
        fields_in[field].wait()
        return full[field].astype(F32).T

    def forward(index):
        return copy_of(index, out.at[index], ext.at[index], rows, slots_each, True)

    def backward(index):
        return copy_of(2 * layers + index, back.at[index], ret.at[index], 0, slots_each, True)

    def send_field(index, field):
        out[index] = dot(pick[...], field).astype(BF16)
        start(forward(index))
        return dot(gather[:, :rows], field)

    def message(index, own):
        finish(forward(index))
        return (own + dot(gather[:, rows:], ext[index, rows:, :])).astype(BF16)

    def send_gradient(index, field):
        back[index] = dot(scatter[rows:, :], field).astype(BF16)
        start(backward(index))
        return dot(scatter[:rows, :], field)

    def returned(index):
        finish(backward(index))
        return dot(put[...], ret[index])

    def weight_part(layer, which, moved, slope):
        square[...] = dot_tn(moved, slope)
        at = (layer * 2 + which) * part
        wpart[at : at + part, :] = square[mine, :]

    used = 2 * layers * part
    if used < wpart.shape[0]:
        wpart[used:, :] = jnp.zeros((wpart.shape[0] - used, channels), F32)

    held[0] = arrived(0)
    out[0] = dot(pick[...], held[0].astype(BF16)).astype(BF16)
    start(forward(0))
    tiles_in.wait()
    for row_block in range(row_blocks):
        row_span = slice(row_block * tile, (row_block + 1) * tile)

        def place(col, carry):
            slot = jnp.int32(0)
            live = jnp.int32(0)
            for k in range(tile_slots):
                hit = (cols_ref[row_block, k] == col) & (mask_ref[row_block, k] > 0)
                slot = jnp.where(hit, k, slot)
                live = jnp.where(hit, 1, live)
            block = tiles_ref[row_block, slot].astype(F32) * live.astype(F32)
            span = pl.ds(pl.multiple_of(col * tile, tile), tile)
            scatter[span, row_span] = block.astype(BF16)
            gather[row_span, span] = block.T.astype(BF16)
            return carry

        lax.fori_loop(0, col_blocks, place, 0)

    held[4] = dot(gather[:, :rows], held[0].astype(BF16))
    put[...] = (lax.broadcasted_iota(jnp.int32, (rows, halo), 0).astype(F32) == slot_row).astype(F32).astype(BF16)
    held[1] = arrived(1)
    held[3] = arrived(3)
    held[2] = arrived(2)
    weights_in.wait()
    moves = 0
    pending = None
    for layer in reversed(range(layers)):
        first = weights_ref[layer, 0]
        second = weights_ref[layer, 1]
        msgs[1] = message(moves, held[4])
        linear_two = dot(msgs[1], second)
        gate_two = sigmoid(linear_two)
        held[5] = gate_two * (1.0 + linear_two * (1.0 - gate_two))
        input_two = (held[1] - linear_two * gate_two).astype(BF16)
        held[1] = input_two.astype(F32)
        held[4] = send_field(moves + 1, input_two)
        if pending is not None:
            held[3] += returned(pending)
        slopes[1] = (held[3] * held[5]).astype(BF16)
        held[2] += send_gradient(moves, dot_nt(slopes[1], second).astype(BF16))
        weight_part(layer, 1, msgs[1], slopes[1])
        msgs[0] = message(moves + 1, held[4])
        linear_one = dot(msgs[0], first)
        gate_one = sigmoid(linear_one)
        held[5] = gate_one * (1.0 + linear_one * (1.0 - gate_one))
        if layer > 0:
            state_one = (held[0] - linear_one * gate_one).astype(BF16)
            held[0] = state_one.astype(F32)
            held[4] = send_field(moves + 2, state_one)
        held[2] += returned(moves)
        slopes[0] = (held[2] * held[5]).astype(BF16)
        held[3] += send_gradient(moves + 1, dot_nt(slopes[0], first).astype(BF16))
        weight_part(layer, 0, msgs[0], slopes[0])
        pending = moves + 1
        moves += 2

    reduce_copy = copy_of(4 * layers, wpart, wsum, 0, rows_each, True)
    start(reduce_copy)
    own_piece = pl.ds(pl.multiple_of(me * rows_each, rows_each), rows_each)
    wsum[own_piece, :] = wpart[own_piece, :]
    wide[...] = held[2].T
    grads_ref[0] = wide[mine, :].astype(BF16)
    finish(reduce_copy)
    total = wsum[:rows_each, :]
    for piece in range(1, blocks):
        total = total + wsum[piece * rows_each : (piece + 1) * rows_each, :]
    wred[...] = total * factor
    spread_copy = copy_of(4 * layers + 1, wred, wall, 0, rows_each, False)
    start(spread_copy)
    wall[own_piece, :] = wred[...]
    wide[...] = (held[3] + returned(pending)).T
    grads_ref[1] = wide[mine, :].astype(BF16)
    finish(spread_copy)
    for layer in range(layers):
        for which in range(2):
            at = (layer * 2 + which) * part
            wgrads_ref[layer, which] = wall[at : at + part, :]


def solution(mesh):
    blocks = mesh.shape["dom"] * mesh.shape["sub"]
    subs = mesh.shape["sub"]
    chans = mesh.shape["chan"]

    def on_device(y_last, dy_last, weights, tile_vals, tile_cols, tile_mask, send_rows, send_count):
        _, part, rows = y_last.shape
        layers = weights.shape[0]
        channels = part * chans
        slots_each = send_rows.shape[2]
        halo = blocks * slots_each
        rows_each = max(8, 2 * layers * part // blocks)
        pieces = blocks * rows_each
        exchanges = 4 * layers + 2
        factor = 1.0 / math.sqrt(rows * blocks)
        vmem = pl.BlockSpec(memory_space=pltpu.VMEM)
        hbm = pl.BlockSpec(memory_space=pl.ANY)
        smem = pl.BlockSpec(memory_space=pltpu.SMEM)
        return pl.pallas_call(
            functools.partial(kernel, blocks, subs, chans, slots_each, rows_each, factor),
            out_shape=(
                jax.ShapeDtypeStruct(y_last.shape, BF16),
                jax.ShapeDtypeStruct((layers, 2, part, channels), F32),
            ),
            in_specs=[hbm, hbm, hbm, hbm, smem, smem, hbm, hbm],
            out_specs=(vmem, vmem),
            scratch_shapes=[
                pltpu.VMEM((4, channels, rows), BF16),
                pltpu.VMEM((rows, rows + halo), BF16),
                pltpu.VMEM((rows + halo, rows), BF16),
                pltpu.VMEM((halo, rows), BF16),
                pltpu.VMEM((rows, halo), BF16),
                pltpu.VMEM((2 * layers, rows + halo, channels), BF16),
                pltpu.VMEM((2 * layers, halo, channels), BF16),
                pltpu.VMEM((2 * layers, halo, channels), BF16),
                pltpu.VMEM((2 * layers, halo, channels), BF16),
                pltpu.VMEM((pieces, channels), F32),
                pltpu.VMEM((pieces, channels), F32),
                pltpu.VMEM((rows_each, channels), F32),
                pltpu.VMEM((pieces, channels), F32),
                pltpu.VMEM((channels, channels), F32),
                pltpu.VMEM((channels, rows), F32),
                pltpu.VMEM((6, rows, channels), F32),
                pltpu.VMEM((2, rows, channels), BF16),
                pltpu.VMEM((2, rows, channels), BF16),
                pltpu.VMEM(weights.shape, BF16),
                pltpu.VMEM(tile_vals.shape, BF16),
                pltpu.VMEM(send_rows.shape, jnp.int32),
                pltpu.VMEM(send_count.shape, jnp.int32),
                pltpu.SemaphoreType.DMA((4, chans)),
                pltpu.SemaphoreType.DMA((4, chans)),
                pltpu.SemaphoreType.DMA((exchanges, blocks)),
                pltpu.SemaphoreType.DMA((exchanges, blocks)),
                pltpu.SemaphoreType.DMA((8,)),
            ],
            compiler_params=pltpu.CompilerParams(
                collective_id=0, has_side_effects=True, vmem_limit_bytes=60 * 1024 * 1024
            ),
        )(y_last, dy_last, weights, tile_vals, tile_cols, tile_mask, send_rows, send_count)

    return jax.shard_map(
        on_device,
        mesh=mesh,
        in_specs=(
            P(None, "chan", ("groups", "dom", "sub")),
            P(None, "chan", ("groups", "dom", "sub")),
            P(),
            P(("groups", "dom", "sub"), None, None, None),
            P(("groups", "dom", "sub"), None),
            P(("groups", "dom", "sub"), None),
            P(("groups", "dom", "sub"), None, None),
            P(("groups", "dom", "sub"), None),
        ),
        out_specs=(P(None, "chan", ("groups", "dom", "sub")), P("groups", None, "chan", None)),
        check_vma=False,
    )
```

```python
import functools
import math

import jax
import jax.numpy as jnp
from jax import lax
from jax.experimental import pallas as pl
from jax.experimental.pallas import tpu as pltpu
from jax.sharding import PartitionSpec as P

MESH = pl.DeviceIdType.MESH
F32 = jnp.float32
BF16 = jnp.bfloat16


def sigmoid(value):
    return 1.0 / (1.0 + jnp.exp(-value))


def dot(a, b):
    return jnp.dot(a, b, preferred_element_type=F32)


def dot_nt(a, b):
    return lax.dot_general(a, b, (((1,), (1,)), ((), ())), preferred_element_type=F32)


def dot_tn(a, b):
    return lax.dot_general(a, b, (((0,), (0,)), ((), ())), preferred_element_type=F32)


def kernel(
    blocks, subs, chans, slots_each, rows_each, factor,
    y_hbm, dy_hbm, weights_hbm, tiles_hbm, cols_ref, mask_ref, rows_hbm, count_hbm,
    grads_ref, wgrads_ref,
    full, gather, scatter, pick, put, ext, out, back, ret, wpart, wsum, wred, wall, square, wide, held, msgs, slopes,
    weights_ref, tiles_ref, rows_ref, count_ref, chan_send, chan_recv, send_sem, recv_sem, local_sem,
):
    layers = weights_ref.shape[0]
    _, part, rows = y_hbm.shape
    channels = part * chans
    row_blocks, tile_slots = cols_ref.shape
    tile = tiles_ref.shape[-1]
    col_blocks = ext.shape[1] // tile
    my_sub = lax.axis_index("sub")
    me = lax.axis_index("dom") * subs + my_sub
    my_chan = lax.axis_index("chan")

    def block_of(step):
        peer = lax.rem(me + step, blocks)
        return peer, {"dom": peer // subs, "sub": lax.rem(peer, subs)}

    def chan_of(step):
        return {"chan": lax.rem(my_chan + step, chans)}

    mine = pl.ds(pl.multiple_of(my_chan * part, part), part)

    def source_of(field):
        return y_hbm.at[field] if field < 2 else dy_hbm.at[field - 2]

    rows_in = pltpu.make_async_copy(rows_hbm, rows_ref, local_sem.at[0])
    count_in = pltpu.make_async_copy(count_hbm, count_ref, local_sem.at[1])
    tiles_in = pltpu.make_async_copy(tiles_hbm, tiles_ref, local_sem.at[2])
    weights_in = pltpu.make_async_copy(weights_hbm, weights_ref, local_sem.at[3])
    fields_in = [
        pltpu.make_async_copy(source_of(field), full.at[field, mine], local_sem.at[4 + field])
        for field in range(4)
    ]
    for copy in (rows_in, count_in, *fields_in, tiles_in, weights_in):
        copy.start()

    barrier = pltpu.get_barrier_semaphore()

    @pl.loop(1, blocks)
    def _(step):
        pl.semaphore_signal(barrier, inc=1, device_id=block_of(step)[1], device_id_type=MESH)

    for step in range(1, chans):
        pl.semaphore_signal(barrier, inc=1, device_id=chan_of(step), device_id_type=MESH)
    pl.semaphore_wait(barrier, blocks - 1 + chans - 1)

    def chan_copy(field, step):
        return pltpu.make_async_remote_copy(
            src_ref=source_of(field),
            dst_ref=full.at[field, mine],
            send_sem=chan_send.at[field, step],
            recv_sem=chan_recv.at[field, step],
            device_id=chan_of(step),
            device_id_type=MESH,
        )

    order = (0, 1, 3, 2)
    for field in order:
        for step in range(1, chans):
            chan_copy(field, step).start()

    def copy_of(index, source, target, offset, size, spread):
        def one(step):
            peer, device = block_of(step)
            src = source.at[pl.ds(pl.multiple_of(peer * size, size), size)] if spread else source
            return pltpu.make_async_remote_copy(
                src_ref=src,
                dst_ref=target.at[pl.ds(pl.multiple_of(offset + me * size, size), size)],
                send_sem=send_sem.at[index, step],
                recv_sem=recv_sem.at[index, step],
                device_id=device,
                device_id_type=MESH,
            )

        return one

    def start(one):
        @pl.loop(1, blocks, unroll=3)
        def _(step):
            one(step).start()

    def finish(one):
        @pl.loop(1, blocks, unroll=3)
        def _(step):
            one(step).wait()

    own_slots = pl.ds(pl.multiple_of(me * slots_each, slots_each), slots_each)
    own_extended = pl.ds(pl.multiple_of(rows + me * slots_each, slots_each), slots_each)
    blank = jnp.zeros((slots_each, channels), BF16)
    for index in range(2 * layers):
        ext[index, own_extended, :] = blank
        ret[index, own_slots, :] = blank

    halo = blocks * slots_each
    rows_in.wait()
    count_in.wait()
    slot_at = lax.broadcasted_iota(jnp.int32, (blocks, halo), 1)
    block_at = lax.broadcasted_iota(jnp.int32, (blocks, halo), 0)
    offset = slot_at - block_at * slots_each
    inside = (offset >= 0) & (offset < slots_each)
    within = jnp.sum(jnp.where(inside, offset, 0).astype(F32), axis=0, keepdims=True)
    spread = inside.astype(F32).astype(BF16)
    entry = lax.broadcasted_iota(jnp.int32, (slots_each, halo), 0).astype(F32)
    matching = (entry == within).astype(F32).astype(BF16)
    listed = rows_ref[0]
    high = dot((listed >> 8).astype(F32).astype(BF16), matching)
    low = dot((listed & 255).astype(F32).astype(BF16), matching)
    chosen = jnp.sum(jnp.where(inside, high * 256.0 + low, 0.0), axis=0, keepdims=True)
    counts = jnp.broadcast_to(count_ref[...].astype(F32), (8, blocks)).astype(BF16)
    limit = dot(counts, spread)[0:1]
    slot_row = jnp.where(within < limit, chosen, -1.0)
    for at in range(0, halo, tile):
        column = jnp.broadcast_to(slot_row[:, at : at + tile], (tile, tile)).T
        for row_at in range(0, rows, tile):
            lanes = (lax.broadcasted_iota(jnp.int32, (tile, tile), 1) + row_at).astype(F32)
            pick[at : at + tile, row_at : row_at + tile] = (lanes == column).astype(F32).astype(BF16)

    def arrived(field):
        for step in range(1, chans):
            chan_copy(field, step).wait()
        fields_in[field].wait()
        return full[field].astype(F32).T

    def forward(index):
        return copy_of(index, out.at[index], ext.at[index], rows, slots_each, True)

    def backward(index):
        return copy_of(2 * layers + index, back.at[index], ret.at[index], 0, slots_each, True)

    def send_field(index, field):
        out[index] = dot(pick[...], field).astype(BF16)
        start(forward(index))
        return dot(gather[:, :rows], field)

    def message(index, own):
        finish(forward(index))
        return (own + dot(gather[:, rows:], ext[index, rows:, :])).astype(BF16)

    def send_gradient(index, field):
        back[index] = dot(scatter[rows:, :], field).astype(BF16)
        start(backward(index))
        return dot(scatter[:rows, :], field)

    def returned(index):
        finish(backward(index))
        return dot(put[...], ret[index])

    def weight_part(layer, which, moved, slope):
        square[...] = dot_tn(moved, slope)
        wpart[layer, which * part : (which + 1) * part, :] = square[mine, :]

    used = 2 * part
    spare = wpart.shape[1] - used
    if spare:
        wpart[:, used:, :] = jnp.zeros((layers, spare, channels), F32)
    own_piece = pl.ds(pl.multiple_of(me * rows_each, rows_each), rows_each)

    def reduce_of(layer):
        return copy_of(4 * layers + layer, wpart.at[layer], wsum.at[layer], 0, rows_each, True)

    def spread_of(layer):
        return copy_of(5 * layers + layer, wred.at[layer], wall.at[layer], 0, rows_each, False)

    def start_reduce(layer):
        start(reduce_of(layer))
        wsum[layer, own_piece, :] = wpart[layer, own_piece, :]

    def start_spread(layer):
        finish(reduce_of(layer))
        total = wsum[layer, :rows_each, :]
        for piece in range(1, blocks):
            total = total + wsum[layer, piece * rows_each : (piece + 1) * rows_each, :]
        wred[layer] = total * factor
        start(spread_of(layer))
        wall[layer, own_piece, :] = wred[layer]


    held[0] = arrived(0)
    out[0] = dot(pick[...], held[0].astype(BF16)).astype(BF16)
    start(forward(0))
    tiles_in.wait()
    for row_block in range(row_blocks):
        row_span = slice(row_block * tile, (row_block + 1) * tile)

        def place(col, carry):
            slot = jnp.int32(0)
            live = jnp.int32(0)
            for k in range(tile_slots):
                hit = (cols_ref[row_block, k] == col) & (mask_ref[row_block, k] > 0)
                slot = jnp.where(hit, k, slot)
                live = jnp.where(hit, 1, live)
            block = tiles_ref[row_block, slot].astype(F32) * live.astype(F32)
            span = pl.ds(pl.multiple_of(col * tile, tile), tile)
            scatter[span, row_span] = block.astype(BF16)
            gather[row_span, span] = block.T.astype(BF16)
            return carry

        lax.fori_loop(0, col_blocks, place, 0)

    held[4] = dot(gather[:, :rows], held[0].astype(BF16))
    put[...] = (lax.broadcasted_iota(jnp.int32, (rows, halo), 0).astype(F32) == slot_row).astype(F32).astype(BF16)
    held[1] = arrived(1)
    held[3] = arrived(3)
    held[2] = arrived(2)
    weights_in.wait()
    moves = 0
    pending = None
    for layer in reversed(range(layers)):
        first = weights_ref[layer, 0]
        second = weights_ref[layer, 1]
        msgs[1] = message(moves, held[4])
        linear_two = dot(msgs[1], second)
        gate_two = sigmoid(linear_two)
        held[5] = gate_two * (1.0 + linear_two * (1.0 - gate_two))
        input_two = (held[1] - linear_two * gate_two).astype(BF16)
        held[1] = input_two.astype(F32)
        held[4] = send_field(moves + 1, input_two)
        if pending is not None:
            held[3] += returned(pending)
        slopes[1] = (held[3] * held[5]).astype(BF16)
        held[2] += send_gradient(moves, dot_nt(slopes[1], second).astype(BF16))
        weight_part(layer, 1, msgs[1], slopes[1])
        if pending is not None:
            start_spread(layer + 1)
        msgs[0] = message(moves + 1, held[4])
        linear_one = dot(msgs[0], first)
        gate_one = sigmoid(linear_one)
        held[5] = gate_one * (1.0 + linear_one * (1.0 - gate_one))
        if layer > 0:
            state_one = (held[0] - linear_one * gate_one).astype(BF16)
            held[0] = state_one.astype(F32)
            held[4] = send_field(moves + 2, state_one)
        held[2] += returned(moves)
        slopes[0] = (held[2] * held[5]).astype(BF16)
        held[3] += send_gradient(moves + 1, dot_nt(slopes[0], first).astype(BF16))
        weight_part(layer, 0, msgs[0], slopes[0])
        start_reduce(layer)
        pending = moves + 1
        moves += 2

    wide[...] = held[2].T
    grads_ref[0] = wide[mine, :].astype(BF16)
    start_spread(0)
    wide[...] = (held[3] + returned(pending)).T
    grads_ref[1] = wide[mine, :].astype(BF16)
    for layer in reversed(range(layers)):
        finish(spread_of(layer))
        for which in range(2):
            wgrads_ref[layer, which] = wall[layer, which * part : (which + 1) * part, :]


def solution(mesh):
    blocks = mesh.shape["dom"] * mesh.shape["sub"]
    subs = mesh.shape["sub"]
    chans = mesh.shape["chan"]

    def on_device(y_last, dy_last, weights, tile_vals, tile_cols, tile_mask, send_rows, send_count):
        _, part, rows = y_last.shape
        layers = weights.shape[0]
        channels = part * chans
        slots_each = send_rows.shape[2]
        halo = blocks * slots_each
        rows_each = max(8, 2 * part // blocks)
        pieces = blocks * rows_each
        exchanges = 6 * layers
        factor = 1.0 / math.sqrt(rows * blocks)
        vmem = pl.BlockSpec(memory_space=pltpu.VMEM)
        hbm = pl.BlockSpec(memory_space=pl.ANY)
        smem = pl.BlockSpec(memory_space=pltpu.SMEM)
        return pl.pallas_call(
            functools.partial(kernel, blocks, subs, chans, slots_each, rows_each, factor),
            out_shape=(
                jax.ShapeDtypeStruct(y_last.shape, BF16),
                jax.ShapeDtypeStruct((layers, 2, part, channels), F32),
            ),
            in_specs=[hbm, hbm, hbm, hbm, smem, smem, hbm, hbm],
            out_specs=(vmem, vmem),
            scratch_shapes=[
                pltpu.VMEM((4, channels, rows), BF16),
                pltpu.VMEM((rows, rows + halo), BF16),
                pltpu.VMEM((rows + halo, rows), BF16),
                pltpu.VMEM((halo, rows), BF16),
                pltpu.VMEM((rows, halo), BF16),
                pltpu.VMEM((2 * layers, rows + halo, channels), BF16),
                pltpu.VMEM((2 * layers, halo, channels), BF16),
                pltpu.VMEM((2 * layers, halo, channels), BF16),
                pltpu.VMEM((2 * layers, halo, channels), BF16),
                pltpu.VMEM((layers, pieces, channels), F32),
                pltpu.VMEM((layers, pieces, channels), F32),
                pltpu.VMEM((layers, rows_each, channels), F32),
                pltpu.VMEM((layers, pieces, channels), F32),
                pltpu.VMEM((channels, channels), F32),
                pltpu.VMEM((channels, rows), F32),
                pltpu.VMEM((6, rows, channels), F32),
                pltpu.VMEM((2, rows, channels), BF16),
                pltpu.VMEM((2, rows, channels), BF16),
                pltpu.VMEM(weights.shape, BF16),
                pltpu.VMEM(tile_vals.shape, BF16),
                pltpu.VMEM(send_rows.shape, jnp.int32),
                pltpu.VMEM(send_count.shape, jnp.int32),
                pltpu.SemaphoreType.DMA((4, chans)),
                pltpu.SemaphoreType.DMA((4, chans)),
                pltpu.SemaphoreType.DMA((exchanges, blocks)),
                pltpu.SemaphoreType.DMA((exchanges, blocks)),
                pltpu.SemaphoreType.DMA((8,)),
            ],
            compiler_params=pltpu.CompilerParams(
                collective_id=0, has_side_effects=True, vmem_limit_bytes=60 * 1024 * 1024
            ),
        )(y_last, dy_last, weights, tile_vals, tile_cols, tile_mask, send_rows, send_count)

    return jax.shard_map(
        on_device,
        mesh=mesh,
        in_specs=(
            P(None, "chan", ("groups", "dom", "sub")),
            P(None, "chan", ("groups", "dom", "sub")),
            P(),
            P(("groups", "dom", "sub"), None, None, None),
            P(("groups", "dom", "sub"), None),
            P(("groups", "dom", "sub"), None),
            P(("groups", "dom", "sub"), None, None),
            P(("groups", "dom", "sub"), None),
        ),
        out_specs=(P(None, "chan", ("groups", "dom", "sub")), P("groups", None, "chan", None)),
        check_vma=False,
    )
```
